32 devices in a mesh: ab: 4 (over z), cd: 2 (over y), rep: 4 (over x, core).
Axes of the slice: x: 2, y: 2, z: 4, core: 2. Of those that a mesh axis runs over, the one named last changes fastest.
Arguments:
- amplitudes: bfloat16 [4, 512, 8192], P('rep', 'ab', 'cd'), may hold values from -6 to 6
- pair_irrep: int32 [4, 512], P('rep', 'ab'), may hold values from 0 to 7, as said below
- integrals: bfloat16 [2048, 8192], P('ab', 'cd'), may hold values from -0.0625 to 0.0625
- residual_in: bfloat16 [4, 512, 2048], P('rep', None, ('ab', 'cd')), may hold values from -6 to 6
Outputs:
- residual: bfloat16 [4, 512, 2048], P('rep', None, ('ab', 'cd'))
The draws below stay inside these ranges and needn't reach their ends.
Inputs may be any that keep to these rules, and one draw needn't show every extreme that they name: For each j, among the 512 labels pair_irrep(l, j * 128 + t) over all layers l and 0 <= t < 128, exactly half are 0, and in one layer l (drawn) all 128 of them are 0.
All inputs are finite; a program needn't handle non-finite values.
Results may differ from the reference program's by a relative error of at most 0.001.
Values may be sent and summed in bfloat16 or wider, within the bound.
A program may use at most 64 MiB of HBM per device.

```python
import jax
import jax.numpy as jnp
from jax import lax

CD = 8192
IRREPS = 8
PAIR_DEV = 128
LAYERS = 4
PAIRS_L = 512
AB = 2048


def draw_pair_irrep(key, part):
    slab_total = PAIRS_L // PAIR_DEV
    others = (LAYERS - 1) * PAIR_DEV
    needed = LAYERS * PAIR_DEV // 2 - PAIR_DEV
    key_busy, key_pick, key_label = jax.random.split(key, 3)
    busy = jax.random.randint(key_busy, (slab_total,), 0, LAYERS)

    def draw_one(sub_key):
        return jax.random.permutation(sub_key, others)
    picks = jax.vmap(draw_one)(jax.random.split(key_pick, slab_total))
    chosen = picks < needed
    layer_ids = jnp.arange(LAYERS)[:, None]
    within = jnp.arange(PAIR_DEV)[None, :]

    def one_slab(busy_layer, chosen_row):
        shifted = layer_ids - (layer_ids > busy_layer).astype(jnp.int32)
        position = jnp.clip(shifted * PAIR_DEV + within, 0, others - 1)
        return jnp.where(layer_ids == busy_layer, True, chosen_row[position])
    marked = jax.vmap(one_slab)(busy, chosen)
    spare = jax.random.randint(key_label, marked.shape, 1, IRREPS)
    labels = jnp.where(marked, 0, spare)
    return jnp.transpose(labels, (1, 0, 2)).reshape(LAYERS, PAIRS_L).astype(jnp.int32)


def steps_of(stream_key, extent, pieces, least, largest):
    def one(dim, shards_of):
        heights = jax.random.uniform(jax.random.fold_in(jax.random.fold_in(stream_key, 6), dim), (shards_of,), jnp.float32, least / len(pieces), largest / len(pieces))
        return jnp.repeat(jnp.exp(heights), extent[dim] // shards_of).reshape((-1,) + (1,) * (len(extent) - dim - 1))

    loudness = one(*pieces[0])
    for cut in pieces[1:]:
        loudness = loudness * one(*cut)
    return loudness


def normal_values(rng, shape, deviation, reach, pieces=(), kind=jnp.bfloat16):
    drawn = jax.random.normal(rng, shape, jnp.float32) * deviation
    if len(pieces) > 0:
        drawn = steps_of(rng, shape, pieces, -0.22, 0.18) * drawn
    return jnp.clip(drawn, min=-reach, max=reach).astype(kind)


def setup_inputs(seed: int = 0) -> dict:
    splits = jax.random.split(jax.random.key(seed), 5)
    amplitudes = normal_values(splits[0], (LAYERS, PAIRS_L, CD), 1.0, 6.0, ((0, 4), (1, 4), (2, 2)))
    pair_irrep = draw_pair_irrep(jax.random.fold_in(splits[4], 71), 0)
    integrals = normal_values(splits[2], (AB, CD), CD ** -0.5, 0.0625, ((0, 4), (1, 2)))
    residual_in = normal_values(splits[3], (LAYERS, PAIRS_L, AB), 1.0, 6.0, ((0, 4), (2, 8)))
    return {"amplitudes": amplitudes, "pair_irrep": pair_irrep, "integrals": integrals, "residual_in": residual_in}


def reference(amplitudes, pair_irrep, integrals, residual_in):
    def one_layer(inputs):
        layer_amps, layer_labels, layer_res = inputs
        ladder = jnp.dot(layer_amps, integrals.T, preferred_element_type=jnp.float32)
        active = (layer_labels == 0).astype(jnp.float32)[:, None]
        return (layer_res.astype(jnp.float32) + active * ladder).astype(jnp.bfloat16)

    return lax.map(one_layer, (amplitudes, pair_irrep, residual_in))
```

```python
import functools

import jax
import jax.numpy as jnp
from jax import lax
from jax.experimental import pallas as pl
from jax.experimental.pallas import tpu as pltpu
from jax.sharding import PartitionSpec as P

CORES = 2
CHUNKS = 4
F32 = jnp.float32
BF16 = jnp.bfloat16
NT = (((1,), (1,)), ((), ()))


def remote(src, dst, send, recv, peer):
    return pltpu.make_async_remote_copy(
        src_ref=src, dst_ref=dst, send_sem=send, recv_sem=recv,
        device_id=peer, device_id_type=pl.DeviceIdType.MESH,
    )


def kernel(
    nz, nc, nr,
    amp, lab, integ, res_in, out,
    v, res, raw, g, labels, acc, y_in, s1, x_in, full,
    v_sem, res_sem, own_sem, lab_own,
    lab_s, lab_r, ax_s, ax_r, ac_s, ac_r, fw_s, fw_r,
    up_s, dn_s, z_r, lup_s, ldn_s, lz_r,
    y_s, y_r, x_s, x_r, c_s, c_r,
):
    z, c, r = lax.axis_index("ab"), lax.axis_index("cd"), lax.axis_index("rep")
    nh = nr // CORES
    hi, lo = r // CORES, r % CORES
    mate = r + 1 - 2 * lo
    rows = amp.shape[1]
    half = amp.shape[2] // nh
    wide = half // CHUNKS
    kept = nr * rows // 2 // CORES
    cols = integ.shape[0] // nc

    def to_rep(i):
        return {"rep": i}

    def columns(h, q):
        return pl.ds(pl.multiple_of(h * half + q * wide, wide), wide)

    def layer_rows(i):
        return pl.ds(pl.multiple_of(i * rows, rows), rows)

    v_copy = [
        pltpu.make_async_copy(integ.at[:, columns(hi, q)], v.at[q], v_sem.at[q])
        for q in range(CHUNKS)
    ]
    own_copy = [
        pltpu.make_async_copy(
            amp.at[0, :, columns(hi, q)], raw.at[q, layer_rows(r)], own_sem.at[q]
        )
        for q in range(CHUNKS)
    ]
    res_copy = pltpu.make_async_copy(res_in.at[0], res, res_sem)
    lab_copy = pltpu.make_async_copy(lab, labels.at[z, r], lab_own)
    lab_copy.start()
    for q in range(CHUNKS):
        own_copy[q].start()

    barrier = pltpu.get_barrier_semaphore()
    for d in range(1, nr):
        pl.semaphore_signal(
            barrier, inc=1, device_id=to_rep(lax.rem(r + d, nr)),
            device_id_type=pl.DeviceIdType.MESH,
        )
    for d in range(1, nc):
        pl.semaphore_signal(
            barrier, inc=1, device_id={"cd": lax.rem(c + d, nc)},
            device_id_type=pl.DeviceIdType.MESH,
        )

    @pl.when(z > 0)
    def _():
        pl.semaphore_signal(
            barrier, inc=1, device_id={"ab": z - 1}, device_id_type=pl.DeviceIdType.MESH
        )

    @pl.when(z < nz - 1)
    def _():
        pl.semaphore_signal(
            barrier, inc=1, device_id={"ab": z + 1}, device_id_type=pl.DeviceIdType.MESH
        )

    ends = (z == 0).astype(jnp.int32) + (z == nz - 1).astype(jnp.int32)
    pl.semaphore_wait(barrier, nr - 1 + nc - 1 + 2 - ends)

    def lab_out(d):
        peer = lax.rem(r + d, nr)
        return remote(lab, labels.at[z, r], lab_s.at[d], lab_r.at[r], to_rep(peer))

    def lab_in(d):
        src = lax.rem(r + d, nr)
        ref = labels.at[z, src]
        return remote(ref, ref, lab_s.at[d], lab_r.at[src], to_rep(src))

    def amp_out(d, q):
        h = lax.rem(hi + d, nh)
        return remote(
            amp.at[0, :, columns(h, q)], raw.at[q, layer_rows(r)],
            ax_s.at[d, q], ax_r.at[hi, q], to_rep(h * CORES + lo),
        )

    def amp_in(d, q):
        h = lax.rem(hi + d, nh)
        ref = raw.at[q, layer_rows(h * CORES + lo)]
        return remote(ref, ref, ax_s.at[d, q], ax_r.at[h, q], to_rep(h * CORES + lo))

    def mate_out(q):
        return remote(
            amp.at[0, :, columns(hi, q)], raw.at[q, layer_rows(r)],
            ac_s.at[q], ac_r.at[q], to_rep(mate),
        )

    def mate_in(q):
        ref = raw.at[q, layer_rows(mate)]
        return remote(ref, ref, ac_s.at[q], ac_r.at[q], to_rep(mate))

    def fwd_out(d, q):
        h = lax.rem(hi + d, nh)
        ref = raw.at[q, layer_rows(h * CORES + lo)]
        return remote(ref, ref, fw_s.at[d, q], fw_r.at[h, q], to_rep(mate))

    def fwd_in(d, q):
        h = lax.rem(hi + d, nh)
        ref = raw.at[q, layer_rows(h * CORES + 1 - lo)]
        return remote(ref, ref, fw_s.at[d, q], fw_r.at[h, q], to_rep(mate))

    for d in range(1, nr):
        lab_out(d).start()
    for q in range(CHUNKS):
        for d in range(1, nh):
            amp_out(d, q).start()
        mate_out(q).start()
    for q in range(CHUNKS):
        v_copy[q].start()
    res_copy.start()

    def up(b, q):
        ref = g.at[b, q]
        return remote(ref, ref, up_s.at[b, q], z_r.at[b, q], {"ab": z + 1})

    def down(b, q):
        ref = g.at[b, q]
        return remote(ref, ref, dn_s.at[b, q], z_r.at[b, q], {"ab": z - 1})

    def lab_up(b):
        ref = labels.at[b]
        return remote(ref, ref, lup_s.at[b], lz_r.at[b], {"ab": z + 1})

    def lab_down(b):
        ref = labels.at[b]
        return remote(ref, ref, ldn_s.at[b], lz_r.at[b], {"ab": z - 1})

    lane = lax.broadcasted_iota(jnp.int32, (rows, rows), 1)
    sub = lax.broadcasted_iota(jnp.int32, (rows, rows), 0)
    before = (sub < lane).astype(F32).astype(BF16)
    diagonal = sub == lane

    def places(b):
        act = [(labels[b, i] == 0).astype(F32) for i in range(nr)]
        stacked = jnp.concatenate(act + [jnp.zeros((8 - nr % 8, rows), F32)], axis=0)
        within = jnp.dot(stacked.astype(BF16), before, preferred_element_type=F32)
        found, start = [], jnp.zeros((1, 1), F32)
        for i in range(nr):
            found.append(jnp.where(act[i] > 0, within[i:i + 1] + start, -1.0))
            start = start + jnp.sum(act[i], axis=1, keepdims=True)
        return found

    def y_out(b, d):
        to = lax.rem(c + d, nc)
        return remote(
            acc.at[b, pl.ds(pl.multiple_of(to * cols, cols), cols)], y_in.at[b, c],
            y_s.at[b, d], y_r.at[b, c], {"cd": to},
        )

    def y_arrive(b, d):
        src = lax.rem(c + d, nc)
        ref = y_in.at[b, src]
        return remote(ref, ref, y_s.at[b, d], y_r.at[b, src], {"cd": src})

    def x_out(b, d):
        h = lax.rem(hi + d, nh)
        return remote(
            s1.at[b], x_in.at[b, hi], x_s.at[b, d], x_r.at[b, hi], to_rep(h * CORES + lo)
        )

    def x_arrive(b, d):
        h = lax.rem(hi + d, nh)
        ref = x_in.at[b, h]
        return remote(ref, ref, x_s.at[b, d], x_r.at[b, h], to_rep(h * CORES + lo))

    def c_out(b):
        ref = full.at[b, lo]
        return remote(ref, ref, c_s.at[b], c_r.at[b], to_rep(mate))

    def c_arrive(b):
        ref = full.at[b, 1 - lo]
        return remote(ref, ref, c_s.at[b], c_r.at[b], to_rep(mate))

    def multiply(b, q):
        part = lax.dot_general(v[q], g[b, q], NT, preferred_element_type=F32)
        if q == 0:
            acc[b] = part
        else:
            acc[b] += part

    def send_y(b):
        for d in range(1, nc):
            y_out(b, d).start()

    def finish(b, phase):
        if phase == 1:
            mine = acc[b, pl.ds(pl.multiple_of(c * cols, cols), cols)]
            for d in range(1, nc):
                y_arrive(b, d).wait_recv()
                mine = mine + y_in[b, lax.rem(c + d, nc)]
            s1[b] = mine
            for d in range(1, nh):
                x_out(b, d).start()
        if phase == 2:
            total = s1[b]
            for d in range(1, nh):
                x_arrive(b, d).wait_recv()
                total = total + x_in[b, lax.rem(hi + d, nh)]
            full[b, lo] = total
            c_out(b).start()
        if phase == 3:
            found = places(b)
            row = jnp.zeros((1, rows), F32)
            for i in range(nr):
                row = row + jnp.where(r == i, found[i], 0.0)
            column = jnp.sum(jnp.where(diagonal, row, 0.0), axis=1, keepdims=True)
            place = lax.broadcasted_iota(jnp.int32, (rows, kept), 1).astype(F32)
            c_arrive(b).wait_recv()
            added = jnp.zeros((rows, cols), F32)
            for i in range(CORES):
                spread = (place + float(i * kept) == column).astype(F32).astype(BF16)
                left = full[b, i]
                for _ in range(3):
                    piece = left.astype(BF16)
                    left = left - piece.astype(F32)
                    added = added + lax.dot_general(
                        spread, piece, NT, preferred_element_type=F32
                    )
            at = pl.ds(pl.multiple_of(b * rows, rows), rows)
            out[0, at] = (res[at].astype(F32) + added).astype(BF16)

    lab_copy.wait()
    for d in range(1, nr):
        lab_in(d).wait_recv()

    @pl.when(z < nz - 1)
    def _():
        lab_up(z).start()

    @pl.when(z > 0)
    def _():
        lab_down(z).start()

    order = lax.broadcasted_iota(jnp.int32, (kept, rows), 0).astype(F32)
    order = order + (lo * kept).astype(F32)
    pick = jnp.concatenate(
        [(order == p).astype(F32).astype(BF16) for p in places(z)], axis=1
    )
    for q in range(CHUNKS):
        for d in range(1, nh):
            amp_in(d, q).wait_recv()
            fwd_out(d, q).start()
        own_copy[q].wait()
        mate_in(q).wait_recv()
        for d in range(1, nh):
            fwd_in(d, q).wait_recv()
        g[z, q] = jnp.dot(pick, raw[q], preferred_element_type=F32).astype(BF16)

        @pl.when(z < nz - 1)
        def _():
            up(z, q).start()

        @pl.when(z > 0)
        def _():
            down(z, q).start()

        v_copy[q].wait()
        multiply(z, q)
    send_y(z)
    res_copy.wait()

    def stage(s, carry):
        for q in range(CHUNKS):
            @pl.when(z - s >= 0)
            def _():
                b = z - s
                up_like = remote(
                    g.at[b, q], g.at[b, q], up_s.at[b, q], z_r.at[b, q], {"ab": z - 1}
                )
                up_like.wait_recv()

                @pl.when(z < nz - 1)
                def _():
                    up(b, q).start()

                multiply(b, q)

            @pl.when(z + s < nz)
            def _():
                b = z + s
                down_like = remote(
                    g.at[b, q], g.at[b, q], dn_s.at[b, q], z_r.at[b, q], {"ab": z + 1}
                )
                down_like.wait_recv()

                @pl.when(z > 0)
                def _():
                    down(b, q).start()

                multiply(b, q)

            if q == 0:
                @pl.when(z - s >= 0)
                def _():
                    b = z - s
                    remote(
                        labels.at[b], labels.at[b], lup_s.at[b], lz_r.at[b], {"ab": z - 1}
                    ).wait_recv()

                    @pl.when(z < nz - 1)
                    def _():
                        lab_up(b).start()

                @pl.when(z + s < nz)
                def _():
                    b = z + s
                    remote(
                        labels.at[b], labels.at[b], ldn_s.at[b], lz_r.at[b], {"ab": z + 1}
                    ).wait_recv()

                    @pl.when(z > 0)
                    def _():
                        lab_down(b).start()
            else:
                @pl.when(z - s + 1 >= 0)
                def _():
                    finish(z - s + 1, q)

                @pl.when((z + s - 1 < nz) & (s > 1))
                def _():
                    finish(z + s - 1, q)

        @pl.when(z - s >= 0)
        def _():
            send_y(z - s)

        @pl.when(z + s < nz)
        def _():
            send_y(z + s)

        return carry

    lax.fori_loop(1, nz, stage, 0)

    @pl.when((z == 0) | (z == nz - 1))
    def _():
        b = nz - 1 - z
        for phase in (1, 2, 3):
            finish(b, phase)

    for d in range(1, nr):
        lab_out(d).wait_send()
    for q in range(CHUNKS):
        for d in range(1, nh):
            amp_out(d, q).wait_send()
            fwd_out(d, q).wait_send()
        mate_out(q).wait_send()

    def drain(b, carry):
        @pl.when((b <= z) & (z < nz - 1))
        def _():
            lab_up(b).wait_send()
            for q in range(CHUNKS):
                up(b, q).wait_send()

        @pl.when((b >= z) & (z > 0))
        def _():
            lab_down(b).wait_send()
            for q in range(CHUNKS):
                down(b, q).wait_send()

        for d in range(1, nc):
            y_out(b, d).wait_send()
        for d in range(1, nh):
            x_out(b, d).wait_send()
        c_out(b).wait_send()
        return carry

    lax.fori_loop(0, nz, drain, 0)


def local(nz, nc, nr, amplitudes, pair_irrep, integrals, residual_in):
    _, rows, wide = amplitudes.shape
    nh = nr // CORES
    chunk = wide // nh // CHUNKS
    height = integrals.shape[0]
    cols = height // nc
    kept = nr * rows // 2 // CORES
    dma = pltpu.SemaphoreType.DMA
    vmem = pltpu.VMEM
    flops = 2 * nz * height * kept * chunk * CHUNKS
    return pl.pallas_call(
        functools.partial(kernel, nz, nc, nr),
        out_shape=jax.ShapeDtypeStruct(residual_in.shape, BF16),
        in_specs=[pl.BlockSpec(memory_space=pl.ANY)] * 4,
        out_specs=pl.BlockSpec(memory_space=pltpu.VMEM),
        scratch_shapes=[
            vmem((CHUNKS, height, chunk), BF16),
            vmem(residual_in.shape[1:], BF16),
            vmem((CHUNKS, nr * rows, chunk), BF16),
            vmem((nz, CHUNKS, kept, chunk), BF16),
            vmem((nz, nr, 1, rows), jnp.int32),
            vmem((nz, height, kept), F32),
            vmem((nz, nc, cols, kept), F32),
            vmem((nz, cols, kept), F32),
            vmem((nz, nh, cols, kept), F32),
            vmem((nz, CORES, cols, kept), F32),
            dma((CHUNKS,)), dma, dma((CHUNKS,)), dma,
            dma((nr,)), dma((nr,)),
            dma((nh, CHUNKS)), dma((nh, CHUNKS)),
            dma((CHUNKS,)), dma((CHUNKS,)),
            dma((nh, CHUNKS)), dma((nh, CHUNKS)),
            dma((nz, CHUNKS)), dma((nz, CHUNKS)), dma((nz, CHUNKS)),
            dma((nz,)), dma((nz,)), dma((nz,)),
            dma((nz, nc)), dma((nz, nc)),
            dma((nz, nh)), dma((nz, nh)),
            dma((nz,)), dma((nz,)),
        ],
        compiler_params=pltpu.CompilerParams(
            collective_id=0, has_side_effects=True, vmem_limit_bytes=48 * 2 ** 20
        ),
        cost_estimate=pl.CostEstimate(
            flops=flops, bytes_accessed=2 * height * wide, transcendentals=0
        ),
    )(amplitudes, pair_irrep, integrals, residual_in)


def solution(mesh):
    return jax.shard_map(
        functools.partial(local, mesh.shape["ab"], mesh.shape["cd"], mesh.shape["rep"]),
        mesh=mesh,
        in_specs=(
            P("rep", "ab", "cd"),
            P("rep", "ab"),
            P("ab", "cd"),
            P("rep", None, ("ab", "cd")),
        ),
        out_specs=P("rep", None, ("ab", "cd")),
        check_vma=False,
    )
```

```python
import functools

import jax
import jax.numpy as jnp
from jax import lax
from jax.experimental import pallas as pl
from jax.experimental.pallas import tpu as pltpu
from jax.sharding import PartitionSpec as P

CORES = 2
CHUNKS = 4
SPLIT = 2
F32 = jnp.float32
BF16 = jnp.bfloat16
NT = (((1,), (1,)), ((), ()))


def remote(src, dst, send, recv, peer):
    return pltpu.make_async_remote_copy(
        src_ref=src, dst_ref=dst, send_sem=send, recv_sem=recv,
        device_id=peer, device_id_type=pl.DeviceIdType.MESH,
    )


def kernel(
    nz, nc, nr,
    amp, lab, integ, res_in, out,
    v, res, raw, g, labels, acc, y_in, s1, x_in, full,
    v_sem, res_sem, own_sem, lab_own,
    lab_s, lab_r, ax_s, ax_r, ac_s, ac_r, fw_s, fw_r,
    up_s, dn_s, z_r, lup_s, ldn_s, lz_r,
    y_s, y_r, x_s, x_r, c_s, c_r,
):
    z, c, r = lax.axis_index("ab"), lax.axis_index("cd"), lax.axis_index("rep")
    nh = nr // CORES
    hi, lo = r // CORES, r % CORES
    mate = r + 1 - 2 * lo
    rows = amp.shape[1]
    half = amp.shape[2] // nh
    wide = half // CHUNKS
    kept = nr * rows // 2 // CORES
    cols = integ.shape[0] // nc
    part = cols // SPLIT

    def to_rep(i):
        return {"rep": i}

    def columns(h, q):
        return pl.ds(pl.multiple_of(h * half + q * wide, wide), wide)

    def layer_rows(i):
        return pl.ds(pl.multiple_of(i * rows, rows), rows)

    v_copy = [
        pltpu.make_async_copy(integ.at[:, columns(hi, q)], v.at[q], v_sem.at[q])
        for q in range(CHUNKS)
    ]
    own_copy = [
        pltpu.make_async_copy(
            amp.at[0, :, columns(hi, q)], raw.at[q, layer_rows(r)], own_sem.at[q]
        )
        for q in range(CHUNKS)
    ]
    res_copy = pltpu.make_async_copy(res_in.at[0], res, res_sem)
    lab_copy = pltpu.make_async_copy(lab, labels.at[z, r], lab_own)
    lab_copy.start()
    for q in range(CHUNKS):
        own_copy[q].start()

    barrier = pltpu.get_barrier_semaphore()
    for d in range(1, nr):
        pl.semaphore_signal(
            barrier, inc=1, device_id=to_rep(lax.rem(r + d, nr)),
            device_id_type=pl.DeviceIdType.MESH,
        )
    for d in range(1, nc):
        pl.semaphore_signal(
            barrier, inc=1, device_id={"cd": lax.rem(c + d, nc)},
            device_id_type=pl.DeviceIdType.MESH,
        )

    @pl.when(z > 0)
    def _():
        pl.semaphore_signal(
            barrier, inc=1, device_id={"ab": z - 1}, device_id_type=pl.DeviceIdType.MESH
        )

    @pl.when(z < nz - 1)
    def _():
        pl.semaphore_signal(
            barrier, inc=1, device_id={"ab": z + 1}, device_id_type=pl.DeviceIdType.MESH
        )

    ends = (z == 0).astype(jnp.int32) + (z == nz - 1).astype(jnp.int32)
    pl.semaphore_wait(barrier, nr - 1 + nc - 1 + 2 - ends)

    def lab_out(d):
        peer = lax.rem(r + d, nr)
        return remote(lab, labels.at[z, r], lab_s.at[d], lab_r.at[r], to_rep(peer))

    def lab_in(d):
        src = lax.rem(r + d, nr)
        ref = labels.at[z, src]
        return remote(ref, ref, lab_s.at[d], lab_r.at[src], to_rep(src))

    def amp_out(d, q):
        h = lax.rem(hi + d, nh)
        return remote(
            amp.at[0, :, columns(h, q)], raw.at[q, layer_rows(r)],
            ax_s.at[d, q], ax_r.at[hi, q], to_rep(h * CORES + lo),
        )

    def amp_in(d, q):
        h = lax.rem(hi + d, nh)
        ref = raw.at[q, layer_rows(h * CORES + lo)]
        return remote(ref, ref, ax_s.at[d, q], ax_r.at[h, q], to_rep(h * CORES + lo))

    def mate_out(q):
        return remote(
            amp.at[0, :, columns(hi, q)], raw.at[q, layer_rows(r)],
            ac_s.at[q], ac_r.at[q], to_rep(mate),
        )

    def mate_in(q):
        ref = raw.at[q, layer_rows(mate)]
        return remote(ref, ref, ac_s.at[q], ac_r.at[q], to_rep(mate))

    def fwd_out(d, q):
        h = lax.rem(hi + d, nh)
        ref = raw.at[q, layer_rows(h * CORES + lo)]
        return remote(ref, ref, fw_s.at[d, q], fw_r.at[h, q], to_rep(mate))

    def fwd_in(d, q):
        h = lax.rem(hi + d, nh)
        ref = raw.at[q, layer_rows(h * CORES + 1 - lo)]
        return remote(ref, ref, fw_s.at[d, q], fw_r.at[h, q], to_rep(mate))

    for d in range(1, nr):
        lab_out(d).start()
    for q in range(CHUNKS):
        for d in range(1, nh):
            amp_out(d, q).start()
        mate_out(q).start()
    for q in range(CHUNKS):
        v_copy[q].start()
    res_copy.start()

    def up(b, q):
        ref = g.at[b, q]
        return remote(ref, ref, up_s.at[b, q], z_r.at[b, q], {"ab": z + 1})

    def down(b, q):
        ref = g.at[b, q]
        return remote(ref, ref, dn_s.at[b, q], z_r.at[b, q], {"ab": z - 1})

    def lab_up(b):
        ref = labels.at[b]
        return remote(ref, ref, lup_s.at[b], lz_r.at[b], {"ab": z + 1})

    def lab_down(b):
        ref = labels.at[b]
        return remote(ref, ref, ldn_s.at[b], lz_r.at[b], {"ab": z - 1})

    lane = lax.broadcasted_iota(jnp.int32, (rows, rows), 1)
    sub = lax.broadcasted_iota(jnp.int32, (rows, rows), 0)
    before = (sub < lane).astype(F32).astype(BF16)
    diagonal = sub == lane

    def places(b):
        act = [(labels[b, i] == 0).astype(F32) for i in range(nr)]
        stacked = jnp.concatenate(act + [jnp.zeros((8 - nr % 8, rows), F32)], axis=0)
        within = jnp.dot(stacked.astype(BF16), before, preferred_element_type=F32)
        found, start = [], jnp.zeros((1, 1), F32)
        for i in range(nr):
            found.append(jnp.where(act[i] > 0, within[i:i + 1] + start, -1.0))
            start = start + jnp.sum(act[i], axis=1, keepdims=True)
        return found

    def y_out(b, d, k):
        to = lax.rem(c + d, nc)
        at = pl.ds(pl.multiple_of(to * cols + k * part, part), part)
        return remote(
            acc.at[b, at], y_in.at[b, c, pl.ds(k * part, part)],
            y_s.at[b, d, k], y_r.at[b, c, k], {"cd": to},
        )

    def y_arrive(b, d, k):
        src = lax.rem(c + d, nc)
        ref = y_in.at[b, src, pl.ds(k * part, part)]
        return remote(ref, ref, y_s.at[b, d, k], y_r.at[b, src, k], {"cd": src})

    def x_out(b, d, k):
        h = lax.rem(hi + d, nh)
        return remote(
            s1.at[b, pl.ds(k * part, part)], x_in.at[b, hi, pl.ds(k * part, part)],
            x_s.at[b, d, k], x_r.at[b, hi, k], to_rep(h * CORES + lo),
        )

    def x_arrive(b, d, k):
        h = lax.rem(hi + d, nh)
        ref = x_in.at[b, h, pl.ds(k * part, part)]
        return remote(ref, ref, x_s.at[b, d, k], x_r.at[b, h, k], to_rep(h * CORES + lo))

    def c_out(b, k):
        ref = full.at[b, lo, pl.ds(k * part, part)]
        return remote(ref, ref, c_s.at[b, k], c_r.at[b, k], to_rep(mate))

    def c_arrive(b, k):
        ref = full.at[b, 1 - lo, pl.ds(k * part, part)]
        return remote(ref, ref, c_s.at[b, k], c_r.at[b, k], to_rep(mate))

    def multiply(b, q):
        part = lax.dot_general(v[q], g[b, q], NT, preferred_element_type=F32)
        if q == 0:
            acc[b] = part
        else:
            acc[b] += part

    def send_y(b):
        for k in range(SPLIT):
            for d in range(1, nc):
                y_out(b, d, k).start()

    def finish(b, phase):
        if phase == 1:
            for k in range(SPLIT):
                at = pl.ds(pl.multiple_of(c * cols + k * part, part), part)
                mine = acc[b, at]
                for d in range(1, nc):
                    y_arrive(b, d, k).wait_recv()
                    mine = mine + y_in[b, lax.rem(c + d, nc), pl.ds(k * part, part)]
                s1[b, pl.ds(k * part, part)] = mine
                for d in range(1, nh):
                    x_out(b, d, k).start()
        if phase == 2:
            for k in range(SPLIT):
                total = s1[b, pl.ds(k * part, part)]
                for d in range(1, nh):
                    x_arrive(b, d, k).wait_recv()
                    total = total + x_in[b, lax.rem(hi + d, nh), pl.ds(k * part, part)]
                full[b, lo, pl.ds(k * part, part)] = total
                c_out(b, k).start()
        if phase == 3:
            found = places(b)
            row = jnp.zeros((1, rows), F32)
            for i in range(nr):
                row = row + jnp.where(r == i, found[i], 0.0)
            column = jnp.sum(jnp.where(diagonal, row, 0.0), axis=1, keepdims=True)
            place = lax.broadcasted_iota(jnp.int32, (rows, kept), 1).astype(F32)
            for k in range(SPLIT):
                c_arrive(b, k).wait_recv()
            added = jnp.zeros((rows, cols), F32)
            for i in range(CORES):
                spread = (place + float(i * kept) == column).astype(F32).astype(BF16)
                left = full[b, i]
                for _ in range(3):
                    piece = left.astype(BF16)
                    left = left - piece.astype(F32)
                    added = added + lax.dot_general(
                        spread, piece, NT, preferred_element_type=F32
                    )
            at = pl.ds(pl.multiple_of(b * rows, rows), rows)
            out[0, at] = (res[at].astype(F32) + added).astype(BF16)

    lab_copy.wait()
    for d in range(1, nr):
        lab_in(d).wait_recv()

    @pl.when(z < nz - 1)
    def _():
        lab_up(z).start()

    @pl.when(z > 0)
    def _():
        lab_down(z).start()

    order = lax.broadcasted_iota(jnp.int32, (kept, rows), 0).astype(F32)
    order = order + (lo * kept).astype(F32)
    pick = jnp.concatenate(
        [(order == p).astype(F32).astype(BF16) for p in places(z)], axis=1
    )
    for q in range(CHUNKS):
        for d in range(1, nh):
            amp_in(d, q).wait_recv()
            fwd_out(d, q).start()
        own_copy[q].wait()
        mate_in(q).wait_recv()
        for d in range(1, nh):
            fwd_in(d, q).wait_recv()
        g[z, q] = jnp.dot(pick, raw[q], preferred_element_type=F32).astype(BF16)

        @pl.when(z < nz - 1)
        def _():
            up(z, q).start()

        @pl.when(z > 0)
        def _():
            down(z, q).start()

        v_copy[q].wait()
        multiply(z, q)
    send_y(z)
    res_copy.wait()

    def stage(s, carry):
        for q in range(CHUNKS):
            @pl.when(z - s >= 0)
            def _():
                b = z - s
                up_like = remote(
                    g.at[b, q], g.at[b, q], up_s.at[b, q], z_r.at[b, q], {"ab": z - 1}
                )
                up_like.wait_recv()

                @pl.when(z < nz - 1)
                def _():
                    up(b, q).start()

                multiply(b, q)

            @pl.when(z + s < nz)
            def _():
                b = z + s
                down_like = remote(
                    g.at[b, q], g.at[b, q], dn_s.at[b, q], z_r.at[b, q], {"ab": z + 1}
                )
                down_like.wait_recv()

                @pl.when(z > 0)
                def _():
                    down(b, q).start()

                multiply(b, q)

            if q == 0:
                @pl.when(z - s >= 0)
                def _():
                    b = z - s
                    remote(
                        labels.at[b], labels.at[b], lup_s.at[b], lz_r.at[b], {"ab": z - 1}
                    ).wait_recv()

                    @pl.when(z < nz - 1)
                    def _():
                        lab_up(b).start()

                @pl.when(z + s < nz)
                def _():
                    b = z + s
                    remote(
                        labels.at[b], labels.at[b], ldn_s.at[b], lz_r.at[b], {"ab": z + 1}
                    ).wait_recv()

                    @pl.when(z > 0)
                    def _():
                        lab_down(b).start()
            else:
                @pl.when(z - s + 1 >= 0)
                def _():
                    finish(z - s + 1, q)

                @pl.when((z + s - 1 < nz) & (s > 1))
                def _():
                    finish(z + s - 1, q)

        @pl.when(z - s >= 0)
        def _():
            send_y(z - s)

        @pl.when(z + s < nz)
        def _():
            send_y(z + s)

        return carry

    lax.fori_loop(1, nz, stage, 0)

    @pl.when((z == 0) | (z == nz - 1))
    def _():
        b = nz - 1 - z
        for phase in (1, 2, 3):
            finish(b, phase)

    for d in range(1, nr):
        lab_out(d).wait_send()
    for q in range(CHUNKS):
        for d in range(1, nh):
            amp_out(d, q).wait_send()
            fwd_out(d, q).wait_send()
        mate_out(q).wait_send()

    def drain(b, carry):
        @pl.when((b <= z) & (z < nz - 1))
        def _():
            lab_up(b).wait_send()
            for q in range(CHUNKS):
                up(b, q).wait_send()

        @pl.when((b >= z) & (z > 0))
        def _():
            lab_down(b).wait_send()
            for q in range(CHUNKS):
                down(b, q).wait_send()

        for k in range(SPLIT):
            for d in range(1, nc):
                y_out(b, d, k).wait_send()
            for d in range(1, nh):
                x_out(b, d, k).wait_send()
            c_out(b, k).wait_send()
        return carry

    lax.fori_loop(0, nz, drain, 0)


def local(nz, nc, nr, amplitudes, pair_irrep, integrals, residual_in):
    _, rows, wide = amplitudes.shape
    nh = nr // CORES
    chunk = wide // nh // CHUNKS
    height = integrals.shape[0]
    cols = height // nc
    kept = nr * rows // 2 // CORES
    dma = pltpu.SemaphoreType.DMA
    vmem = pltpu.VMEM
    flops = 2 * nz * height * kept * chunk * CHUNKS
    return pl.pallas_call(
        functools.partial(kernel, nz, nc, nr),
        out_shape=jax.ShapeDtypeStruct(residual_in.shape, BF16),
        in_specs=[pl.BlockSpec(memory_space=pltpu.HBM)] * 4,
        out_specs=pl.BlockSpec(memory_space=pltpu.VMEM),
        scratch_shapes=[
            vmem((CHUNKS, height, chunk), BF16),
            vmem(residual_in.shape[1:], BF16),
            vmem((CHUNKS, nr * rows, chunk), BF16),
            vmem((nz, CHUNKS, kept, chunk), BF16),
            vmem((nz, nr, 1, rows), jnp.int32),
            vmem((nz, height, kept), F32),
            vmem((nz, nc, cols, kept), F32),
            vmem((nz, cols, kept), F32),
            vmem((nz, nh, cols, kept), F32),
            vmem((nz, CORES, cols, kept), F32),
            dma((CHUNKS,)), dma, dma((CHUNKS,)), dma,
            dma((nr,)), dma((nr,)),
            dma((nh, CHUNKS)), dma((nh, CHUNKS)),
            dma((CHUNKS,)), dma((CHUNKS,)),
            dma((nh, CHUNKS)), dma((nh, CHUNKS)),
            dma((nz, CHUNKS)), dma((nz, CHUNKS)), dma((nz, CHUNKS)),
            dma((nz,)), dma((nz,)), dma((nz,)),
            dma((nz, nc, SPLIT)), dma((nz, nc, SPLIT)),
            dma((nz, nh, SPLIT)), dma((nz, nh, SPLIT)),
            dma((nz, SPLIT)), dma((nz, SPLIT)),
        ],
        compiler_params=pltpu.CompilerParams(
            collective_id=0, has_side_effects=True, vmem_limit_bytes=62 * 2 ** 20
        ),
        cost_estimate=pl.CostEstimate(
            flops=flops, bytes_accessed=2 * height * wide, transcendentals=0
        ),
    )(amplitudes, pair_irrep, integrals, residual_in)


def solution(mesh):
    return jax.shard_map(
        functools.partial(local, mesh.shape["ab"], mesh.shape["cd"], mesh.shape["rep"]),
        mesh=mesh,
        in_specs=(
            P("rep", "ab", "cd"),
            P("rep", "ab"),
            P("ab", "cd"),
            P("rep", None, ("ab", "cd")),
        ),
        out_specs=P("rep", None, ("ab", "cd")),
        check_vma=False,
    )
```

```python
import functools

import jax
import jax.numpy as jnp
from jax import lax
from jax.experimental import pallas as pl
from jax.experimental.pallas import tpu as pltpu
from jax.sharding import PartitionSpec as P

CORES = 2
CHUNKS = 4
SPLIT = 2
F32 = jnp.float32
BF16 = jnp.bfloat16
NT = (((1,), (1,)), ((), ()))


def remote(src, dst, send, recv, peer):
    return pltpu.make_async_remote_copy(
        src_ref=src, dst_ref=dst, send_sem=send, recv_sem=recv,
        device_id=peer, device_id_type=pl.DeviceIdType.MESH,
    )


def kernel(
    nz, nc, nr,
    amp, lab, integ, res_in, out,
    v, res, raw, g, labels, acc, y_in, s1, x_in, full,
    v_sem, res_sem, own_sem, lab_own,
    lab_s, lab_r, ax_s, ax_r, ac_s, ac_r, fw_s, fw_r,
    up_s, dn_s, z_r, lup_s, ldn_s, lz_r,
    y_s, y_r, x_s, x_r, c_s, c_r,
):
    z, c, r = lax.axis_index("ab"), lax.axis_index("cd"), lax.axis_index("rep")
    nh = nr // CORES
    hi, lo = r // CORES, r % CORES
    mate = r + 1 - 2 * lo
    rows = amp.shape[1]
    half = amp.shape[2] // nh
    wide = half // CHUNKS
    kept = nr * rows // 2 // CORES
    cols = integ.shape[0] // nc
    part = cols // SPLIT

    def to_rep(i):
        return {"rep": i}

    def columns(h, q):
        return pl.ds(pl.multiple_of(h * half + q * wide, wide), wide)

    def layer_rows(i):
        return pl.ds(pl.multiple_of(i * rows, rows), rows)

    v_copy = [
        pltpu.make_async_copy(integ.at[:, columns(hi, q)], v.at[q], v_sem.at[q])
        for q in range(CHUNKS)
    ]
    own_copy = [
        pltpu.make_async_copy(
            amp.at[0, :, columns(hi, q)], raw.at[q, layer_rows(r)], own_sem.at[q]
        )
        for q in range(CHUNKS)
    ]
    res_copy = pltpu.make_async_copy(res_in.at[0], res, res_sem)
    lab_copy = pltpu.make_async_copy(lab, labels.at[z, r], lab_own)
    lab_copy.start()
    for q in range(CHUNKS):
        own_copy[q].start()

    barrier = pltpu.get_barrier_semaphore()
    for d in range(1, nr):
        pl.semaphore_signal(
            barrier, inc=1, device_id=to_rep(lax.rem(r + d, nr)),
            device_id_type=pl.DeviceIdType.MESH,
        )
    for d in range(1, nc):
        pl.semaphore_signal(
            barrier, inc=1, device_id={"cd": lax.rem(c + d, nc)},
            device_id_type=pl.DeviceIdType.MESH,
        )

    @pl.when(z > 0)
    def _():
        pl.semaphore_signal(
            barrier, inc=1, device_id={"ab": z - 1}, device_id_type=pl.DeviceIdType.MESH
        )

    @pl.when(z < nz - 1)
    def _():
        pl.semaphore_signal(
            barrier, inc=1, device_id={"ab": z + 1}, device_id_type=pl.DeviceIdType.MESH
        )

    ends = (z == 0).astype(jnp.int32) + (z == nz - 1).astype(jnp.int32)
    pl.semaphore_wait(barrier, nr - 1 + nc - 1 + 2 - ends)

    def lab_out(d):
        peer = lax.rem(r + d, nr)
        return remote(lab, labels.at[z, r], lab_s.at[d], lab_r.at[r], to_rep(peer))

    def lab_in(d):
        src = lax.rem(r + d, nr)
        ref = labels.at[z, src]
        return remote(ref, ref, lab_s.at[d], lab_r.at[src], to_rep(src))

    def amp_out(d, q):
        h = lax.rem(hi + d, nh)
        return remote(
            amp.at[0, :, columns(h, q)], raw.at[q, layer_rows(r)],
            ax_s.at[d, q], ax_r.at[hi, q], to_rep(h * CORES + lo),
        )

    def amp_in(d, q):
        h = lax.rem(hi + d, nh)
        ref = raw.at[q, layer_rows(h * CORES + lo)]
        return remote(ref, ref, ax_s.at[d, q], ax_r.at[h, q], to_rep(h * CORES + lo))

    def mate_out(q):
        return remote(
            amp.at[0, :, columns(hi, q)], raw.at[q, layer_rows(r)],
            ac_s.at[q], ac_r.at[q], to_rep(mate),
        )

    def mate_in(q):
        ref = raw.at[q, layer_rows(mate)]
        return remote(ref, ref, ac_s.at[q], ac_r.at[q], to_rep(mate))

    def fwd_out(d, q):
        h = lax.rem(hi + d, nh)
        ref = raw.at[q, layer_rows(h * CORES + lo)]
        return remote(ref, ref, fw_s.at[d, q], fw_r.at[h, q], to_rep(mate))

    def fwd_in(d, q):
        h = lax.rem(hi + d, nh)
        ref = raw.at[q, layer_rows(h * CORES + 1 - lo)]
        return remote(ref, ref, fw_s.at[d, q], fw_r.at[h, q], to_rep(mate))

    for d in range(1, nr):
        lab_out(d).start()
    for q in range(CHUNKS):
        for d in range(1, nh):
            amp_out(d, q).start()
        mate_out(q).start()
    for q in range(CHUNKS):
        v_copy[q].start()
    res_copy.start()

    def up(b, q):
        ref = g.at[b, q]
        return remote(ref, ref, up_s.at[b, q], z_r.at[b, q], {"ab": z + 1})

    def down(b, q):
        ref = g.at[b, q]
        return remote(ref, ref, dn_s.at[b, q], z_r.at[b, q], {"ab": z - 1})

    def lab_up(b):
        ref = labels.at[b]
        return remote(ref, ref, lup_s.at[b], lz_r.at[b], {"ab": z + 1})

    def lab_down(b):
        ref = labels.at[b]
        return remote(ref, ref, ldn_s.at[b], lz_r.at[b], {"ab": z - 1})

    lane = lax.broadcasted_iota(jnp.int32, (rows, rows), 1)
    sub = lax.broadcasted_iota(jnp.int32, (rows, rows), 0)
    before = (sub < lane).astype(F32).astype(BF16)
    diagonal = sub == lane

    def places(b):
        act = [(labels[b, i] == 0).astype(F32) for i in range(nr)]
        stacked = jnp.concatenate(act + [jnp.zeros((8 - nr % 8, rows), F32)], axis=0)
        within = jnp.dot(stacked.astype(BF16), before, preferred_element_type=F32)
        found, start = [], jnp.zeros((1, 1), F32)
        for i in range(nr):
            found.append(jnp.where(act[i] > 0, within[i:i + 1] + start, -1.0))
            start = start + jnp.sum(act[i], axis=1, keepdims=True)
        return found

    def y_out(b, d, k):
        to = lax.rem(c + d, nc)
        at = pl.ds(pl.multiple_of(to * cols + k * part, part), part)
        return remote(
            acc.at[b, at], y_in.at[b, c, pl.ds(k * part, part)],
            y_s.at[b, d, k], y_r.at[b, c, k], {"cd": to},
        )

    def y_arrive(b, d, k):
        src = lax.rem(c + d, nc)
        ref = y_in.at[b, src, pl.ds(k * part, part)]
        return remote(ref, ref, y_s.at[b, d, k], y_r.at[b, src, k], {"cd": src})

    def x_out(b, d, k):
        h = lax.rem(hi + d, nh)
        return remote(
            s1.at[b, pl.ds(k * part, part)], x_in.at[b, hi, pl.ds(k * part, part)],
            x_s.at[b, d, k], x_r.at[b, hi, k], to_rep(h * CORES + lo),
        )

    def x_arrive(b, d, k):
        h = lax.rem(hi + d, nh)
        ref = x_in.at[b, h, pl.ds(k * part, part)]
        return remote(ref, ref, x_s.at[b, d, k], x_r.at[b, h, k], to_rep(h * CORES + lo))

    def c_out(b, k):
        ref = full.at[b, lo, pl.ds(k * part, part)]
        return remote(ref, ref, c_s.at[b, k], c_r.at[b, k], to_rep(mate))

    def c_arrive(b, k):
        ref = full.at[b, 1 - lo, pl.ds(k * part, part)]
        return remote(ref, ref, c_s.at[b, k], c_r.at[b, k], to_rep(mate))

    def multiply(b, q):
        part = lax.dot_general(v[q], g[b, q], NT, preferred_element_type=F32)
        if q == 0:
            acc[b] = part
        else:
            acc[b] += part

    def send_y(b):
        for k in range(SPLIT):
            for d in range(1, nc):
                y_out(b, d, k).start()

    def finish(b, phase):
        if phase == 1:
            for k in range(SPLIT):
                at = pl.ds(pl.multiple_of(c * cols + k * part, part), part)
                mine = acc[b, at]
                for d in range(1, nc):
                    y_arrive(b, d, k).wait_recv()
                    mine = mine + y_in[b, lax.rem(c + d, nc), pl.ds(k * part, part)]
                s1[b, pl.ds(k * part, part)] = mine
                for d in range(1, nh):
                    x_out(b, d, k).start()
        if phase == 2:
            for k in range(SPLIT):
                total = s1[b, pl.ds(k * part, part)]
                for d in range(1, nh):
                    x_arrive(b, d, k).wait_recv()
                    total = total + x_in[b, lax.rem(hi + d, nh), pl.ds(k * part, part)]
                full[b, lo, pl.ds(k * part, part)] = total
                c_out(b, k).start()
        if phase == 3:
            found = places(b)
            row = jnp.zeros((1, rows), F32)
            for i in range(nr):
                row = row + jnp.where(r == i, found[i], 0.0)
            column = jnp.sum(jnp.where(diagonal, row, 0.0), axis=1, keepdims=True)
            place = lax.broadcasted_iota(jnp.int32, (rows, kept), 1).astype(F32)
            for k in range(SPLIT):
                c_arrive(b, k).wait_recv()
            added = jnp.zeros((rows, cols), F32)
            for i in range(CORES):
                spread = (place + float(i * kept) == column).astype(F32).astype(BF16)
                left = full[b, i]
                for _ in range(3):
                    piece = left.astype(BF16)
                    left = left - piece.astype(F32)
                    added = added + lax.dot_general(
                        spread, piece, NT, preferred_element_type=F32
                    )
            at = pl.ds(pl.multiple_of(b * rows, rows), rows)
            out[0, at] = (res[at].astype(F32) + added).astype(BF16)

    lab_copy.wait()
    for d in range(1, nr):
        lab_in(d).wait_recv()

    @pl.when(z < nz - 1)
    def _():
        lab_up(z).start()

    @pl.when(z > 0)
    def _():
        lab_down(z).start()

    order = lax.broadcasted_iota(jnp.int32, (kept, rows), 0).astype(F32)
    order = order + (lo * kept).astype(F32)
    pick = jnp.concatenate(
        [(order == p).astype(F32).astype(BF16) for p in places(z)], axis=1
    )
    for q in range(CHUNKS):
        for d in range(1, nh):
            amp_in(d, q).wait_recv()
            fwd_out(d, q).start()
        own_copy[q].wait()
        mate_in(q).wait_recv()
        for d in range(1, nh):
            fwd_in(d, q).wait_recv()
        g[z, q] = jnp.dot(pick, raw[q], preferred_element_type=F32).astype(BF16)

        @pl.when(z < nz - 1)
        def _():
            up(z, q).start()

        @pl.when(z > 0)
        def _():
            down(z, q).start()

        v_copy[q].wait()
        multiply(z, q)
    send_y(z)
    res_copy.wait()

    def stage(s, carry):
        for q in range(CHUNKS):
            @pl.when(z - s >= 0)
            def _():
                b = z - s
                up_like = remote(
                    g.at[b, q], g.at[b, q], up_s.at[b, q], z_r.at[b, q], {"ab": z - 1}
                )
                up_like.wait_recv()

                @pl.when(z < nz - 1)
                def _():
                    up(b, q).start()

                multiply(b, q)

            @pl.when(z + s < nz)
            def _():
                b = z + s
                down_like = remote(
                    g.at[b, q], g.at[b, q], dn_s.at[b, q], z_r.at[b, q], {"ab": z + 1}
                )
                down_like.wait_recv()

                @pl.when(z > 0)
                def _():
                    down(b, q).start()

                multiply(b, q)

            if q == 0:
                @pl.when(z - s >= 0)
                def _():
                    b = z - s
                    remote(
                        labels.at[b], labels.at[b], lup_s.at[b], lz_r.at[b], {"ab": z - 1}
                    ).wait_recv()

                    @pl.when(z < nz - 1)
                    def _():
                        lab_up(b).start()

                @pl.when(z + s < nz)
                def _():
                    b = z + s
                    remote(
                        labels.at[b], labels.at[b], ldn_s.at[b], lz_r.at[b], {"ab": z + 1}
                    ).wait_recv()

                    @pl.when(z > 0)
                    def _():
                        lab_down(b).start()
            else:
                @pl.when(z - s + 1 >= 0)
                def _():
                    finish(z - s + 1, q)

                @pl.when((z + s - 1 < nz) & (s > 1))
                def _():
                    finish(z + s - 1, q)

        @pl.when(z - s >= 0)
        def _():
            send_y(z - s)

        @pl.when(z + s < nz)
        def _():
            send_y(z + s)

        return carry

    lax.fori_loop(1, nz, stage, 0)

    at_end = (z == 0) | (z == nz - 1)

    def sums_left(b):
        for k in range(SPLIT):
            for d in range(1, nc):
                y_out(b, d, k).wait_send()
            for d in range(1, nh):
                x_out(b, d, k).wait_send()
            c_out(b, k).wait_send()

    for d in range(1, nr):
        lab_out(d).wait_send()
    for q in range(CHUNKS):
        for d in range(1, nh):
            amp_out(d, q).wait_send()
            fwd_out(d, q).wait_send()
        mate_out(q).wait_send()

    def drain(b, carry):
        @pl.when((b <= z) & (z < nz - 1))
        def _():
            lab_up(b).wait_send()
            for q in range(CHUNKS):
                up(b, q).wait_send()

        @pl.when((b >= z) & (z > 0))
        def _():
            lab_down(b).wait_send()
            for q in range(CHUNKS):
                down(b, q).wait_send()

        @pl.when(~at_end | (b != nz - 1 - z))
        def _():
            sums_left(b)

        return carry

    lax.fori_loop(0, nz, drain, 0)

    @pl.when(at_end)
    def _():
        b = nz - 1 - z
        for phase in (1, 2, 3):
            finish(b, phase)
        sums_left(b)


def local(nz, nc, nr, amplitudes, pair_irrep, integrals, residual_in):
    _, rows, wide = amplitudes.shape
    nh = nr // CORES
    chunk = wide // nh // CHUNKS
    height = integrals.shape[0]
    cols = height // nc
    kept = nr * rows // 2 // CORES
    dma = pltpu.SemaphoreType.DMA
    vmem = pltpu.VMEM
    flops = 2 * nz * height * kept * chunk * CHUNKS
    return pl.pallas_call(
        functools.partial(kernel, nz, nc, nr),
        out_shape=jax.ShapeDtypeStruct(residual_in.shape, BF16),
        in_specs=[pl.BlockSpec(memory_space=pltpu.HBM)] * 4,
        out_specs=pl.BlockSpec(memory_space=pltpu.VMEM),
        scratch_shapes=[
            vmem((CHUNKS, height, chunk), BF16),
            vmem(residual_in.shape[1:], BF16),
            vmem((CHUNKS, nr * rows, chunk), BF16),
            vmem((nz, CHUNKS, kept, chunk), BF16),
            vmem((nz, nr, 1, rows), jnp.int32),
            vmem((nz, height, kept), F32),
            vmem((nz, nc, cols, kept), F32),
            vmem((nz, cols, kept), F32),
            vmem((nz, nh, cols, kept), F32),
            vmem((nz, CORES, cols, kept), F32),
            dma((CHUNKS,)), dma, dma((CHUNKS,)), dma,
            dma((nr,)), dma((nr,)),
            dma((nh, CHUNKS)), dma((nh, CHUNKS)),
            dma((CHUNKS,)), dma((CHUNKS,)),
            dma((nh, CHUNKS)), dma((nh, CHUNKS)),
            dma((nz, CHUNKS)), dma((nz, CHUNKS)), dma((nz, CHUNKS)),
            dma((nz,)), dma((nz,)), dma((nz,)),
            dma((nz, nc, SPLIT)), dma((nz, nc, SPLIT)),
            dma((nz, nh, SPLIT)), dma((nz, nh, SPLIT)),
            dma((nz, SPLIT)), dma((nz, SPLIT)),
        ],
        compiler_params=pltpu.CompilerParams(
            collective_id=0, has_side_effects=True, vmem_limit_bytes=62 * 2 ** 20
        ),
        cost_estimate=pl.CostEstimate(
            flops=flops, bytes_accessed=2 * height * wide, transcendentals=0
        ),
    )(amplitudes, pair_irrep, integrals, residual_in)


def solution(mesh):
    return jax.shard_map(
        functools.partial(local, mesh.shape["ab"], mesh.shape["cd"], mesh.shape["rep"]),
        mesh=mesh,
        in_specs=(
            P("rep", "ab", "cd"),
            P("rep", "ab"),
            P("ab", "cd"),
            P("rep", None, ("ab", "cd")),
        ),
        out_specs=P("rep", None, ("ab", "cd")),
        check_vma=False,
    )
```
